1024 devices in a mesh: scen: 8 (over z_hi, x), shard: 128 (over y, z_lo, core).
Axes of the slice: x: 4, y: 8, z: 16 (z_hi: 2, z_lo: 8; z = z_hi * 8 + z_lo), core: 2. Of those that a mesh axis runs over, the one named last changes fastest.
Arguments:
- layer_input: bfloat16 [262144, 1024], P(('scen', 'shard')), may hold values from -24 to 24
- grad_output: bfloat16 [262144, 1024], P(('scen', 'shard')), may hold values from -6 to 6
- row_counts: int32 [8, 128], P('scen', 'shard'), may hold values from 32 to 256, as said below
- w_shared: bfloat16 [1024, 1024], replicated, may hold values from -0.1875 to 0.1875
- w_scen: bfloat16 [8, 1024, 1024], P('scen'), may hold values from 0.099609375 to 1.8984375
- gain_shared: float32 [1024], replicated, may hold values from 0.25 to 1.75
- gain_scen: float32 [8, 1024], P('scen'), may hold values from 0.25 to 1.75
- saved_mean: float32 [8, 1024], P('scen'), may hold values from -3 to 3
- saved_rstd: float32 [8, 1024], P('scen'), may hold values from 0.5 to 2
- bag_lengths: int32 [1024, 256], P(('scen', 'shard')), may hold values from 1 to 4, 320 in all within a row
- owner_shard: int32 [327680, 1], P(('scen', 'shard')), may hold values from 0 to 127; in each aligned block of 320 rows (0 to 319, 320 to 639, ...) at most 3 rows name the same one
- table_row: int32 [327680], P(('scen', 'shard')), may hold values from 0 to 511
Outputs:
- grad_input: bfloat16 [262144, 1024], P(('scen', 'shard'))
- dw_shared: float32 [1024, 1024], P('shard')
- dw_scen: float32 [8, 1024, 1024], P('scen', 'shard')
- dgain_shared: float32 [1024], replicated
- dgain_scen: float32 [8, 1024], P('scen')
- table_grad: float32 [65536, 128], P('shard')
The draws below stay inside these ranges and needn't reach their ends.
Inputs may be any that keep to these rules, and one draw needn't show every extreme that they name: `row_counts`: at least 32 live rows on every device; some device holds 256. `bag_lengths`: each of a device's 256 bags holds at least one entry; they sum to 320. `owner_shard`: among the entries of one device no owner appears more than 3 times.
All inputs are finite; a program needn't handle non-finite values.
Results may differ from the reference program's by a relative error of at most 0.015.
Values may be sent and summed in bfloat16 or wider, within the bound.
A program may use at most 64 MiB of HBM per device.

```python
import math
import jax
import jax.numpy as jnp
import numpy as np
from jax import lax

DIN = 1024
DOUT = 1024
EMB = 128
ROWS_DEV = 256
TROWS_DEV = 512
SCEN = 8
ROWS = 262144
ENT_DEV = 320
ENTS = 327680
CAP = 3
N_SCEN = 8
N_SHARD = 128


def draw_row_counts(key, part):
    key = jax.random.fold_in(key, 7)
    key_drop, key_pick = jax.random.split(key, 2)
    shard_pos = jnp.arange(N_SHARD, dtype=jnp.int32)
    base_count = ROWS_DEV // 4 + 3 * ROWS_DEV // 4 * shard_pos // max(N_SHARD - 1, 1)
    dropped = jax.random.randint(key_drop, (SCEN, N_SHARD), 0, ROWS_DEV // 8 + 1)
    counts = jnp.maximum(base_count[None, :] - dropped, ROWS_DEV // 8)
    chosen = jax.random.randint(key_pick, (), 0, SCEN)
    fullest = (jnp.arange(SCEN, dtype=jnp.int32)[:, None] == chosen) & (shard_pos[None, :] == N_SHARD - 1)
    return jnp.where(fullest, ROWS_DEV, counts).astype(jnp.int32)


def with_ends(result, stream_key, smallest, largest):
    longest = result.shape.index(max(result.shape))
    spots = []
    for shift in (0, 1):
        where = [jax.random.randint(jax.random.fold_in(stream_key, axis), (), 0, length) for axis, length in enumerate(result.shape)]
        where[longest] = (where[longest] + shift) % result.shape[longest]
        spots.append(tuple(where))
    return result.at[spots[0]].set(smallest).at[spots[1]].set(largest)


def with_spikes(entries, stream_key, source, target, parts, factor):
    def block_of(dim):
        return (jnp.arange(entries.shape[dim]) // (entries.shape[dim] // parts)).reshape((-1,) + (1,) * (entries.ndim - 1 - dim))

    one_side = jax.random.permutation(stream_key, parts)[block_of(target)]
    far = (block_of(target) + parts // 2) % parts
    return jnp.where((block_of(source) == one_side) | (block_of(source) == far), factor * entries, entries)


def steps_of(own_key, extent, shards, least, largest):
    gain = 1.0
    for position, shards_of in shards:
        steps = jax.random.uniform(jax.random.fold_in(jax.random.fold_in(own_key, 6), position), (shards_of,), jnp.float32, least / len(shards), largest / len(shards))
        gain = gain * jnp.repeat(jnp.exp(steps), extent[position] // shards_of).reshape((-1,) + (1,) * (len(extent) - 1 - position))
    return gain


def split_up(amount, total, most, slope):
    weights = [(1 << 20) // math.isqrt(standing ** slope) + 1 for standing in range(2, amount + 1)]
    rest, holding = total - most - (amount - 1), [1] * (amount - 1)
    while rest > 0:
        candidates = [i for i in range(amount - 1) if holding[i] < most]
        mass, left = sum([weights[i] for i in candidates]), rest
        for i in candidates:
            extra = min(most - holding[i], max(1, left * weights[i] // mass), rest)
            holding[i] = holding[i] + extra
            rest = rest - extra
    return np.array([most] + holding)


def uneven(stream_key, count, total, bound, slope):
    if count == 2:
        one = jax.random.randint(stream_key, (), max(1, total - bound), min(bound, total - 1) + 1)
        return jnp.stack([one, total - one])
    tallies = jnp.asarray(split_up(count, total, bound, slope), jnp.int32)
    twos = (count - 1) // 2
    source_of, taker = tallies[1:1 + 2 * twos:2], tallies[2:2 + 2 * twos:2]
    margin = jnp.minimum(source_of - 1, bound - taker)
    moved = jax.random.randint(jax.random.fold_in(stream_key, 1), (twos,), 0, 1 << 20) % (margin + 1)
    tallies = tallies.at[1:1 + 2 * twos:2].set(source_of - moved).at[2:2 + 2 * twos:2].set(taker + moved)
    return tallies[jax.random.permutation(jax.random.fold_in(stream_key, 2), count)]


def assign_block(stream_key, own, number, rows, number_of, top, reach, skew):
    sequence = jax.random.permutation(stream_key, number_of)
    heavy_load, ordinary = load_shares(number_of, rows * top, reach, skew, True), load_shares(number_of, rows * top, reach, skew, False)
    places = jnp.arange(number_of)

    def named(sizes, rotation):
        used = int((sizes > 0).sum())
        fixed = max(1, used // 4)
        passed = fixed + (places - fixed + rotation * (used - fixed)) % max(1, number_of - fixed)
        return jnp.zeros((number_of,), jnp.int32).at[sequence[jnp.where(places < fixed, places, passed)]].set(jnp.asarray(sizes, jnp.int32))

    sizes = jnp.where(number % 4 == 0, named(heavy_load, number // 4), named(ordinary, number - number // 4 - 1))
    mixed = jax.random.permutation(jax.random.fold_in(own, 3), number_of)
    giver, taker = mixed[0:number_of // 2 * 2:2], mixed[1:number_of // 2 * 2:2]
    margin = jnp.minimum(sizes[giver] - 1, reach - sizes[taker]) // 2
    margin = jnp.where((giver == sequence[0]) | (taker == sequence[0]) | (sizes[taker] == 0), 0, jnp.maximum(margin, 0))
    passed = jax.random.randint(jax.random.fold_in(own, 4), (number_of // 2,), 0, 1 << 20) % (margin + 1)
    sizes = sizes.at[giver].add(-passed).at[taker].add(passed)
    members = jnp.searchsorted(jnp.cumsum(sizes), jnp.arange(rows * top), side="right").astype(jnp.int32)
    grid = members.reshape(top, rows).T
    grid = grid[jax.random.permutation(jax.random.fold_in(own, 1), rows)]
    rotation = jax.random.randint(jax.random.fold_in(own, 2), (rows, 1), 0, top)
    return jnp.take_along_axis(grid, (jnp.arange(top)[None, :] + rotation) % top, axis=1)


def load_shares(number_of, total, bound, slope, full):
    portions = [(1 << 20) // math.isqrt(standing ** slope) + 1 for standing in range(1, number_of + 1)]
    largest = bound if full else min(bound, max(-(-total // number_of), total * portions[0] // sum(portions)))
    least = 1 if total - largest >= number_of - 1 else 0
    holding, rest = [largest] + [least] * (number_of - 1), total - largest - least * (number_of - 1)
    while rest > 0:
        candidates = [i for i in range(1, number_of) if holding[i] < largest] or [i for i in range(1, number_of) if holding[i] < bound]
        pool, remaining = sum([portions[i] for i in candidates]), rest
        for i in candidates:
            more = min(bound - holding[i], max(1, remaining * portions[i] // pool), rest)
            holding[i] = holding[i] + more
            rest = rest - more
    return np.array(holding)


def scatter_about(own_key, extent, scale, most, cuts=(), kind=jnp.bfloat16):
    gain = steps_of(own_key, extent, cuts, -0.22, 0.18) if cuts else 1.0
    result = jax.random.normal(own_key, extent, jnp.float32) * scale * gain
    return jnp.minimum(jnp.maximum(result, -most), most).astype(kind)


def heavy_noise(stream_key, extent, spread, bound, cuts, heavy, kind=jnp.bfloat16):
    array = spread * jax.random.normal(stream_key, extent, jnp.float32)
    if cuts:
        array = array * steps_of(stream_key, extent, cuts, -0.22, 0.18)
    return jnp.clip(with_spikes(array, jax.random.fold_in(stream_key, 3), *heavy), -bound, bound).astype(kind)


def setup_inputs(seed: int = 0) -> dict:
    streams_of = jax.random.split(jax.random.key(seed), 13)
    layer_input = heavy_noise(streams_of[0], (ROWS, DIN), 1.0, 24.0, ((0, 1024),), (0, 1, 1024, 6.0))
    grad_output = scatter_about(streams_of[1], (ROWS, DOUT), 1.0, 6.0, ((0, 1024),))
    row_counts = draw_row_counts(jax.random.fold_in(streams_of[12], 71), 0)
    w_shared = scatter_about(streams_of[3], (DIN, DOUT), DIN ** -0.5, 0.1875)
    w_scen = jnp.clip(1.0 + 0.18 * jax.random.normal(streams_of[4], (SCEN, DIN, DOUT), jnp.float32), 0.099609375, 1.8984375).astype(jnp.bfloat16)
    gain_shared = jnp.clip(1.0 + 0.15 * jax.random.normal(streams_of[5], (DOUT,), jnp.float32), 0.25, 1.75)
    gain_scen = jnp.clip(1.0 + 0.15 * jax.random.normal(streams_of[6], (SCEN, DOUT), jnp.float32), 0.25, 1.75)
    saved_mean = scatter_about(streams_of[7], (SCEN, DOUT), 0.5, 3.0, ((0, 8),), jnp.float32)
    saved_rstd = jnp.clip(jnp.exp(math.log(2.0) - 1.3862944 * jax.random.uniform(streams_of[8], (SCEN, DOUT), jnp.float32) ** steps_of(streams_of[8], (SCEN, DOUT), ((0, 8),), -0.2, 0.2)), 0.5, 2.0)
    bag_lengths = jax.vmap(lambda own: uneven(own, ROWS_DEV, ENT_DEV, 4, 1))(jax.random.split(streams_of[9], (N_SCEN * N_SHARD))).reshape((N_SCEN * N_SHARD, ROWS_DEV)).astype(jnp.int32)
    owner_shard_keys = jax.random.split(jax.random.fold_in(streams_of[10], 1), ENTS // ENT_DEV)
    owner_shard_turns = jax.random.permutation(jax.random.fold_in(streams_of[10], 3), ENTS // ENT_DEV)
    owner_shard = jax.vmap(lambda own, number: assign_block(jax.random.fold_in(streams_of[10], 2), own, number, ENT_DEV, N_SHARD, 1, CAP, 2))(owner_shard_keys, owner_shard_turns).reshape((ENTS, 1))
    table_row = with_ends(jax.random.randint(streams_of[11], (ENTS,), 0, TROWS_DEV), jax.random.fold_in(streams_of[11], 1), 0, TROWS_DEV - 1).astype(jnp.int32)
    return dict(layer_input=layer_input, grad_output=grad_output, row_counts=row_counts, w_shared=w_shared, w_scen=w_scen, gain_shared=gain_shared, gain_scen=gain_scen, saved_mean=saved_mean, saved_rstd=saved_rstd, bag_lengths=bag_lengths, owner_shard=owner_shard, table_row=table_row)


def reference(layer_input, grad_output, row_counts, w_shared, w_scen, gain_shared, gain_scen, saved_mean, saved_rstd, bag_lengths, owner_shard, table_row):
    per_scen = ROWS_DEV * N_SHARD
    scen_in = layer_input.reshape(SCEN, per_scen, DIN)
    scen_dy = grad_output.reshape(SCEN, per_scen, DOUT)
    slot_idx = jnp.arange(per_scen, dtype=jnp.int32) % ROWS_DEV
    live_mask = (slot_idx[None, :] < jnp.repeat(row_counts, ROWS_DEV, axis=1)).astype(jnp.float32)

    def per_scenario(packed):
        rows_in, rows_dy, live_s, weight_s, mean_s, rstd_s, gain_s = packed
        w_eff = (w_shared.astype(jnp.float32) * weight_s.astype(jnp.float32)).astype(jnp.bfloat16)
        pre_norm = jnp.dot(rows_in, w_eff, preferred_element_type=jnp.float32)
        normed = (pre_norm - mean_s) * rstd_s
        masked = rows_dy.astype(jnp.float32) * live_s[:, None]
        count_s = jnp.sum(live_s)
        sum_dy = jnp.sum(masked, axis=0)
        sum_dyx = jnp.sum(masked * normed, axis=0)
        gain_prod = gain_shared * gain_s
        grad_pre = (live_s[:, None] * gain_prod * rstd_s * (masked - sum_dy / count_s - normed * sum_dyx / count_s)).astype(jnp.bfloat16)
        grad_in = lax.dot_general(grad_pre, w_eff, (((1,), (1,)), ((), ())), preferred_element_type=jnp.float32).astype(jnp.bfloat16)
        dw_s = lax.dot_general(rows_in, grad_pre, (((0,), (0,)), ((), ())), preferred_element_type=jnp.float32)
        return grad_in, dw_s * w_shared.astype(jnp.float32), dw_s * weight_s.astype(jnp.float32), gain_shared * sum_dyx, gain_s * sum_dyx

    grad_in, dw_scen, shared_terms, dgain_scen, gain_terms = lax.map(per_scenario, (scen_in, scen_dy, live_mask, w_scen, saved_mean, saved_rstd, gain_scen))
    dw_shared = jnp.sum(shared_terms, axis=0)
    dgain_shared = jnp.sum(gain_terms, axis=0)
    grad_input = grad_in.reshape(ROWS, DIN)

    devices_all = SCEN * N_SHARD
    bag_ends = jnp.cumsum(bag_lengths, axis=1)
    entry_ids = jnp.arange(ENT_DEV, dtype=jnp.int32)
    bag_of = jnp.sum((bag_ends[:, None, :] <= entry_ids[None, :, None]).astype(jnp.int32), axis=2)
    source_row = (jnp.arange(devices_all, dtype=jnp.int32)[:, None] * ROWS_DEV + bag_of).reshape(-1)
    entry_vals = grad_input[source_row, :EMB].astype(jnp.float32)
    target_row = owner_shard[:, 0] * TROWS_DEV + table_row
    table_grad = jax.ops.segment_sum(entry_vals, target_row, num_segments=N_SHARD * TROWS_DEV)
    return grad_input, dw_shared, dw_scen, dgain_shared, dgain_scen, table_grad
```

```python
import jax
import jax.numpy as jnp
from jax import lax
from jax.experimental import pallas as pl
from jax.experimental.pallas import tpu as pltpu
from jax.sharding import PartitionSpec as P

F32, BF16, I32 = jnp.float32, jnp.bfloat16, jnp.int32
NZH, NX, NY, NZ = 2, 4, 8, 8
ROWS, DIN, DOUT, EMB, TROWS, ENT, CAP = 256, 1024, 1024, 128, 512, 320, 3
HALF = DOUT // 2
LOAD = 256
PART = NZ * CAP
SLOT = 2 * PART
SLOTS = NY * SLOT
TBLK = TROWS // NX
LONG = NY // 2


def remote(src, dst, send, recv, dev):
    return pltpu.make_async_remote_copy(
        src_ref=src,
        dst_ref=dst,
        send_sem=send,
        recv_sem=recv,
        device_id=dev,
        device_id_type=pl.DeviceIdType.MESH,
    )


class Spread:
    def __init__(self, n, me, dev, src_of, buf, sems):
        self.n, self.me, self.dev, self.src_of, self.buf = n, me, dev, src_of, buf
        self.send, self.recv = sems

    def start(self):
        for k in range(1, self.n):
            p = lax.rem(self.me + k, self.n)
            remote(self.src_of(p), self.buf.at[self.me], self.send.at[k], self.recv.at[self.me], self.dev(p)).start()

    def wait(self):
        for k in range(1, self.n):
            q = lax.rem(self.me + k, self.n)
            remote(self.buf.at[q], self.buf.at[q], self.send.at[k], self.recv.at[q], self.dev(q)).wait_recv()

    def finish(self):
        for k in range(1, self.n):
            p = lax.rem(self.me + k, self.n)
            remote(self.src_of(p), self.buf.at[self.me], self.send.at[k], self.recv.at[self.me], self.dev(p)).wait_send()


def nt(a, b):
    return lax.dot_general(a, b, (((1,), (1,)), ((), ())), preferred_element_type=F32)


def nn(a, b):
    return jnp.dot(a, b, preferred_element_type=F32)


def iota(shape, dim):
    return lax.broadcasted_iota(I32, shape, dim)


def hot(cond):
    return jnp.where(cond, 1.0, 0.0).astype(BF16)


def total(buf, n):
    acc = buf[0].astype(F32)
    for i in range(1, n):
        acc = acc + buf[i].astype(F32)
    return acc


def kernel(
    x_hbm, g_hbm, cnt_ref, ws_hbm, wc_hbm, gs_ref, gc_ref, mean_ref, rstd_ref, len_ref, own_ref, row_ref,
    gi_hbm, dws_ref, dwc_ref, dgs_ref, dgc_ref, tab_ref,
    xb, gb, ws, wc, we, nb, gp, xt, gi,
    stat, stat_c, stat_y, stat_z, fin,
    dw, ring, blk, dz, shx, shz,
    meta, meta_p, pick, ids_s, ids_y, ids_t, ids_z, rows_hot, perm,
    val_s, val_y, val_t, val_z, tab_s, tab_x, tab_h, tab_g, dgx, dgh,
    s_load, s_out, s_core, r_core, s_ring, r_ring,
    *spread_sems,
):
    scen, shard = lax.axis_index("scen"), lax.axis_index("shard")
    zh, x = scen // NX, lax.rem(scen, NX)
    y, z, c = shard // (NZ * 2), lax.rem(shard // 2, NZ), lax.rem(shard, 2)

    def dev_y(p):
        return (scen, (p * NZ + z) * 2 + c)

    def dev_z(p):
        return (scen, (y * NZ + p) * 2 + c)

    def dev_x(p):
        return (zh * NX + p, shard)

    def dev_h(p):
        return (p * NX + x, shard)

    other = 1 - c
    partner = (scen, (y * NZ + z) * 2 + other)

    in_x = pltpu.make_async_copy(x_hbm, xb.at[pl.ds(0, ROWS)], s_load.at[0])
    in_g = pltpu.make_async_copy(g_hbm, gb.at[pl.ds(0, ROWS)], s_load.at[1])
    loads = DOUT // LOAD
    in_w = []
    for j in range(loads):
        cols = pl.ds(j * LOAD, LOAD)
        in_w.append((
            pltpu.make_async_copy(ws_hbm.at[:, cols], ws.at[:, cols], s_load.at[2 + 2 * j]),
            pltpu.make_async_copy(wc_hbm.at[:, cols], wc.at[:, cols], s_load.at[3 + 2 * j]),
        ))
    in_x.start()
    for a, b in in_w[:1]:
        a.start()
        b.start()
    in_g.start()
    for a, b in in_w[1:]:
        a.start()
        b.start()

    barrier = pltpu.get_barrier_semaphore()
    peers = [dev_h(1 - zh)]
    peers += [dev_z(lax.rem(z + k, NZ)) for k in range(1, NZ)]
    peers += [dev_y(lax.rem(y + k, NY)) for k in range(1, NY)]
    peers += [dev_x(lax.rem(x + k, NX)) for k in range(1, NX)]
    peers += [partner]
    for p in peers:
        pl.semaphore_signal(barrier, 1, device_id=p, device_id_type=pl.DeviceIdType.MESH)

    sems = [(spread_sems[2 * i], spread_sems[2 * i + 1]) for i in range(len(spread_sems) // 2)]
    go_stat_y = Spread(NY, y, dev_y, lambda p: stat_y.at[y], stat_y, sems[0])
    go_stat_z = Spread(NZ, z, dev_z, lambda p: stat_z.at[z], stat_z, sems[1])
    go_ids_y = Spread(NY, y, dev_y, lambda p: ids_s.at[p], ids_y, sems[2])
    go_ids_z = Spread(NZ, z, dev_z, lambda p: ids_t.at[p], ids_z, sems[3])
    go_val_y = Spread(NY, y, dev_y, lambda p: val_s.at[p], val_y, sems[4])
    go_val_z = Spread(NZ, z, dev_z, lambda p: val_t.at[p], val_z, sems[5])
    go_dw_z = Spread(NZ, z, dev_z, lambda p: blk.at[p], dz, sems[6])
    go_sh_x = Spread(NX, x, dev_x, lambda p: shx.at[x], shx, sems[7])
    go_sh_h = Spread(NZH, zh, dev_h, lambda p: shz.at[zh], shz, sems[8])
    go_tab_x = Spread(NX, x, dev_x, lambda p: tab_s.at[p], tab_x, sems[9])
    go_tab_h = Spread(NZH, zh, dev_h, lambda p: tab_h.at[zh], tab_h, sems[10])
    go_tab_g = Spread(NX, x, dev_x, lambda p: tab_g.at[x], tab_g, sems[11])
    go_dg_x = Spread(NX, x, dev_x, lambda p: dgx.at[x], dgx, sems[12])
    go_dg_h = Spread(NZH, zh, dev_h, lambda p: dgh.at[zh], dgh, sems[13])
    spreads = [go_stat_y, go_stat_z, go_ids_y, go_ids_z, go_val_y, go_val_z, go_dw_z, go_sh_x, go_sh_h,
               go_tab_x, go_tab_h, go_tab_g, go_dg_x, go_dg_h]
    core_stat = remote(stat.at[other], stat_c, s_core.at[0], r_core.at[0], partner)
    core_fin = remote(fin.at[c], fin.at[c], s_core.at[1], r_core.at[1], partner)
    core_fin_in = remote(fin.at[other], fin.at[other], s_core.at[1], r_core.at[1], partner)
    core_meta = remote(meta, meta_p, s_core.at[2], r_core.at[2], partner)
    core_x = remote(x_hbm, xb.at[pl.ds(ROWS, ROWS)], s_core.at[3], r_core.at[3], partner)
    core_g = remote(g_hbm, gb.at[pl.ds(ROWS, ROWS)], s_core.at[4], r_core.at[4], partner)

    own_hot = hot(own_ref[...] == iota((ENT, 128), 1))
    earlier = nn(hot(iota((ENT, ENT), 1) < iota((ENT, ENT), 0)), own_hot) * own_hot.astype(F32)
    place_row = nt(jnp.ones((8, 128), BF16), earlier.astype(BF16))
    owner_row = nt(iota((8, 128), 1).astype(F32).astype(BF16), own_hot)
    meta[...] = jnp.zeros_like(meta)
    meta[0:1, 0:ROWS] = len_ref[...].astype(F32)
    meta[1:2, 0:ENT] = owner_row[0:1] * 4.0 + place_row[0:1]
    meta[2:3, 0:ENT] = row_ref[...].astype(F32)

    count = cnt_ref[0, 0]
    stat[...] = jnp.zeros_like(stat)
    live = iota((ROWS, LOAD), 0) < count
    in_x.wait()
    for j in range(loads):
        cols = pl.ds(j * LOAD, LOAD)
        in_w[j][0].wait()
        in_w[j][1].wait()
        w_j = (ws[:, cols].astype(F32) * wc[:, cols].astype(F32)).astype(BF16)
        we[:, cols] = w_j
        normed = (nn(xb[0:ROWS, :], w_j) - mean_ref[:, cols]) * rstd_ref[:, cols]
        nb[0:ROWS, cols] = normed
        if j == 0:
            in_g.wait()
        masked = jnp.where(live, gb[0:ROWS, cols].astype(F32), 0.0)
        h, at = (j * LOAD) // HALF, (j * LOAD) % HALF
        stat[h, 0:1, at : at + LOAD] = jnp.sum(masked, axis=0, keepdims=True)
        stat[h, 1:2, at : at + LOAD] = jnp.sum(masked * normed, axis=0, keepdims=True)
    cnt_row = jnp.full((1, HALF), count, I32).astype(F32)
    stat[0, 2:3, :] = cnt_row
    stat[1, 2:3, :] = cnt_row

    pl.semaphore_wait(barrier, len(peers))
    core_stat.start()
    core_meta.start()
    core_x.start()
    core_g.start()

    xt_rows = DIN // 2
    choose_i, choose_k = iota((xt_rows, DIN), 0), iota((xt_rows, DIN), 1)
    choose = hot(choose_k == (choose_i >> 3) * 16 + c * 8 + (choose_i & 7))

    core_stat.wait_recv()
    stat_y[y] = stat[c] + stat_c[...]
    go_stat_y.start()

    xt[:, 0:ROWS] = nt(choose, xb[0:ROWS, :]).astype(BF16)

    def slots_of(m, src):
        lens = m[0:1, 0:ROWS]
        upto = hot(iota((ROWS, ROWS), 0) <= iota((ROWS, ROWS), 1))
        ends = nn(jnp.broadcast_to(lens, (8, ROWS)).astype(BF16), upto)[0:1]
        entry = iota((ENT, ROWS), 0).astype(F32)
        picker = hot((ends > entry) & (ends - lens <= entry))
        code = m[1:2, 0:ENT].astype(I32)
        owner, place = code >> 2, code & 3
        inside = src * PART + ((owner >> 1) & 7) * CAP + place
        mine = (owner & 1) == c
        slot = jnp.where(mine, (owner >> 4) * SLOT + inside, -1)
        wide = jnp.where(mine, (owner >> 4) * 128 + inside, -1)
        chosen = nn(hot(iota((SLOTS, ENT), 0) == slot), picker).astype(BF16)
        name = m[2:3, 0:ENT].astype(I32) + 1
        part = jnp.where(iota((8, ENT), 0) == 0, name >> 4, name & 15)
        names = nt(part.astype(F32).astype(BF16), hot(iota((NY * 128, ENT), 0) == wide))
        return chosen, names

    core_meta.wait_recv()
    chosen, names = slots_of(meta, c)
    pick[:, 0:ROWS] = chosen
    chosen, names_p = slots_of(meta_p, other)
    pick[:, ROWS : 2 * ROWS] = chosen
    names = names + names_p
    for i in range(NY):
        ids_s[i] = names[:, i * 128 : (i + 1) * 128]

    go_stat_y.wait()
    stat_z[z] = total(stat_y, NY)
    go_stat_z.start()
    ids_y[y] = ids_s[y]
    go_ids_y.start()

    core_x.wait_recv()
    xt[:, ROWS : 2 * ROWS] = nt(choose, xb[ROWS : 2 * ROWS, :]).astype(BF16)
    for j in range(loads):
        cols = pl.ds(j * LOAD, LOAD)
        nb[ROWS : 2 * ROWS, cols] = (nn(xb[ROWS : 2 * ROWS, :], we[:, cols]) - mean_ref[:, cols]) * rstd_ref[:, cols]
    out_i, in_i = iota((SLOTS, SLOTS), 0), iota((SLOTS, SLOTS), 1)
    to_z = (out_i * 1366) >> 16
    in_z = out_i - to_z * SLOT
    six, from_y = in_z >> 3, in_z & 7
    src_c = jnp.where(six >= CAP, 1, 0)
    perm[...] = hot(in_i == from_y * SLOT + src_c * PART + to_z * CAP + six - CAP * src_c)
    core_g.wait_recv()

    go_stat_z.wait()
    fin[c] = total(stat_z, NZ)
    core_fin.start()
    scale = gs_ref[...] * gc_ref[...] * rstd_ref[...]
    core_fin_in.wait_recv()

    sums = [jnp.concatenate([fin[0, i : i + 1, :], fin[1, i : i + 1, :]], axis=1) for i in range(3)]
    sum_dyx = sums[1]
    mean_dy, mean_dyx = sums[0] / sums[2], sums[1] / sums[2]
    count_p = stat_c[2:3, 0:1]

    step = 64
    for i in range(2 * ROWS // step):
        rows = slice(i * step, (i + 1) * step)
        at = iota((step, 1), 0).astype(F32) + float((i * step) % ROWS)
        if i * step < ROWS:
            alive = at < count.astype(F32)
        else:
            alive = at < count_p
        g = gb[rows, :].astype(F32)
        gp[rows, :] = jnp.where(alive, scale * (g - mean_dy - nb[rows, :] * mean_dyx), 0.0).astype(BF16)

    for j in range(DOUT // LOAD):
        cols = slice(j * LOAD, (j + 1) * LOAD)
        dw[:, :, :, cols] = nn(xt[...], gp[:, cols]).astype(BF16).reshape(NY, 2, 32, LOAD)

    streams = []
    for h in range(2):
        for d in (1, -1):
            streams.append((len(streams), h, d, LONG if (h == 0) == (d == 1) else LONG - 1))

    def hop(s, h, d, n, k):
        src = dw.at[lax.rem(y + d * (n - k) + NY, NY), h] if k == 0 else ring.at[s, k - 1]
        return remote(src, ring.at[s, k], s_ring.at[s, k], r_ring.at[s, k], dev_y(lax.rem(y + d + NY, NY)))

    for s, h, d, n in streams:
        hop(s, h, d, n, 0).start()

    def ring_step(k):
        for s, h, d, n in streams:
            if k < n - 1:
                hop(s, h, d, n, k).wait_recv()
                own = dw[lax.rem(y + d * (n - k - 1) + NY, NY), h]
                ring[s, k] = (ring[s, k].astype(F32) + own.astype(F32)).astype(BF16)
                hop(s, h, d, n, k + 1).start()

    pooled = nt(gp[...], we[0:EMB, :]).astype(BF16)
    val_s[...] = nn(pick[...], pooled).astype(BF16).reshape(NY, SLOT, EMB)
    val_y[y] = val_s[y]
    go_val_y.start()

    dgc_ref[...] = gs_ref[...] * sum_dyx
    gain_term = gc_ref[...] * sum_dyx
    for i in range(8):
        dgx[x, i : i + 1, :] = gain_term[:, i * 128 : (i + 1) * 128]
    go_dg_x.start()

    for j in range(2):
        cols = slice(j * LOAD, (j + 1) * LOAD)
        gi[:, cols] = nt(gp[0:ROWS, :], we[cols, :]).astype(BF16)

    ring_step(0)

    for j in range(2, DIN // LOAD):
        cols = slice(j * LOAD, (j + 1) * LOAD)
        gi[:, cols] = nt(gp[0:ROWS, :], we[cols, :]).astype(BF16)
    out_gi = pltpu.make_async_copy(gi, gi_hbm, s_out.at[0])
    out_gi.start()

    go_ids_y.wait()
    halves = [jnp.concatenate([ids_y[i, r : r + 1, :] for i in range(NY)], axis=0) for r in range(2)]
    q_in, q_out = iota((128, NZ * 128), 0), iota((128, NZ * 128), 1)
    q_z, q_six = q_out >> 7, q_out & 127
    q_src = jnp.where(q_six >= CAP, 1, 0)
    spreader = hot((q_six < 2 * CAP) & (q_in == q_src * PART + q_z * CAP + q_six - CAP * q_src))
    named = nn(jnp.concatenate(halves, axis=0).astype(BF16), spreader)
    named = named[0:8] * 16.0 + named[8:16]
    for i in range(NZ):
        ids_t[i] = named[:, i * 128 : (i + 1) * 128]
    ids_z[z] = ids_t[z]
    go_ids_z.start()

    ring_step(1)

    go_val_y.wait()
    val_t[...] = nn(perm[...], val_y[...].reshape(SLOTS, EMB)).astype(BF16).reshape(NZ, SLOT, EMB)
    val_z[z] = val_t[z]
    go_val_z.start()
    go_dg_x.wait()
    dgh[zh] = total(dgx, NX)
    go_dg_h.start()

    ring_step(2)

    go_ids_z.wait()
    for i in range(NZ):
        for k in range(0, 2 * CAP, 2):
            pair = [ids_z[i][:, t : t + 1] - 1.0 for t in (k, k + 1)]
            at = jnp.concatenate([jnp.broadcast_to(t, (8, TROWS)) for t in pair], axis=0)
            at_row = i * SLOT + k * 8
            rows_hot[at_row : at_row + 16, :] = hot(at == iota((16, TROWS), 1).astype(F32))

    for s, h, d, n in streams:
        hop(s, h, d, n, n - 1).wait_recv()
    for h in range(2):
        long_s, short_s = (0, 1) if h == 0 else (3, 2)
        summed = ring[long_s, LONG - 1].astype(F32) + dw[y, h].astype(F32) + ring[short_s, LONG - 2].astype(F32)
        for i in range(4):
            b = summed[8 * i : 8 * (i + 1)]
            blk[4 * h + i] = jnp.concatenate([b[:, 0:HALF], b[:, HALF:DOUT]], axis=0).astype(BF16)
    dz[z] = blk[z]
    go_dw_z.start()

    go_val_z.wait()
    table = lax.dot_general(
        rows_hot[...], val_z[...].reshape(SLOTS, EMB), (((0,), (0,)), ((), ())), preferred_element_type=F32
    )
    tab_s[...] = table.astype(BF16).reshape(NX, TBLK, EMB)
    tab_x[x] = tab_s[x]
    go_tab_x.start()

    base = pl.multiple_of((y * NZ + z) * 16, 16)

    def block_of(w):
        pair = w[pl.ds(base, 16), :].astype(F32)
        return jnp.where(c == 0, pair[0:8], pair[8:16])

    w_s, w_c = block_of(ws), block_of(wc)

    go_dw_z.wait()
    summed = total(dz, NZ)
    dw_rows = jnp.concatenate([summed[0:8], summed[8:16]], axis=1)
    shared = dw_rows * w_c
    shx[x] = jnp.concatenate([shared[:, 0:HALF], shared[:, HALF:DOUT]], axis=0).astype(BF16)
    go_sh_x.start()
    dwc_ref[...] = dw_rows * w_s

    go_tab_x.wait()
    tab_h[zh] = total(tab_x, NX).astype(BF16)
    go_tab_h.start()

    go_sh_x.wait()
    shz[zh] = total(shx, NX).astype(BF16)
    go_sh_h.start()

    go_dg_h.wait()
    dgs_ref[...] = total(dgh, NZH)

    go_tab_h.wait()
    tab_g[x] = total(tab_h, NZH).astype(BF16)
    go_tab_g.start()

    go_sh_h.wait()
    summed = total(shz, NZH)
    dws_ref[...] = jnp.concatenate([summed[0:8], summed[8:16]], axis=1)

    go_tab_g.wait()
    tab_ref[...] = tab_g[...].astype(F32).reshape(TROWS, EMB)

    for sp in spreads:
        sp.finish()
    for cp in (core_stat, core_fin, core_meta, core_x, core_g):
        cp.wait_send()
    for s, h, d, n in streams:
        for k in range(n):
            hop(s, h, d, n, k).wait_send()
    out_gi.wait()


def per_device(*args):
    (layer_input, grad_output, row_counts, w_shared, w_scen, gain_shared, gain_scen,
     saved_mean, saved_rstd, bag_lengths, owner_shard, table_row) = args
    vm, sm, anywhere = (pl.BlockSpec(memory_space=m) for m in (pltpu.VMEM, pltpu.SMEM, pl.ANY))
    dma = pltpu.SemaphoreType.DMA
    V = pltpu.VMEM
    sizes = [NY, NZ, NY, NZ, NY, NZ, NZ, NX, NZH, NX, NZH, NX, NX, NZH]
    scratch = [
        V((2 * ROWS, DIN), BF16), V((2 * ROWS, DOUT), BF16), V((DIN, DOUT), BF16), V((DIN, DOUT), BF16),
        V((DIN, DOUT), BF16), V((2 * ROWS, DOUT), F32), V((2 * ROWS, DOUT), BF16), V((DIN // 2, 2 * ROWS), BF16),
        V((ROWS, DIN), BF16),
        V((2, 8, HALF), F32), V((8, HALF), F32), V((NY, 8, HALF), F32), V((NZ, 8, HALF), F32), V((2, 8, HALF), F32),
        V((NY, 2, 32, DOUT), BF16), V((4, LONG, 32, DOUT), BF16), V((NZ, 16, HALF), BF16),
        V((NZ, 16, HALF), BF16), V((NX, 16, HALF), BF16), V((NZH, 16, HALF), BF16),
        V((8, 512), F32), V((8, 512), F32), V((SLOTS, 2 * ROWS), BF16), V((NY, 8, 128), F32), V((NY, 8, 128), F32),
        V((NZ, 8, 128), F32), V((NZ, 8, 128), F32), V((SLOTS, TROWS), BF16), V((SLOTS, SLOTS), BF16),
        V((NY, SLOT, EMB), BF16), V((NY, SLOT, EMB), BF16), V((NZ, SLOT, EMB), BF16), V((NZ, SLOT, EMB), BF16),
        V((NX, TBLK, EMB), BF16), V((NX, TBLK, EMB), BF16), V((NZH, TBLK, EMB), BF16), V((NX, TBLK, EMB), BF16),
        V((NX, 8, 128), F32), V((NZH, 8, 128), F32),
        dma((2 + 2 * (DOUT // LOAD),)), dma((1,)), dma((5,)), dma((5,)), dma((4, LONG)), dma((4, LONG)),
    ]
    for n in sizes:
        scratch += [dma((n,)), dma((n,))]
    shape = jax.ShapeDtypeStruct
    grad_in, dw_shared, dw_scen, dgain_shared, dgain_scen, table = pl.pallas_call(
        kernel,
        out_shape=(
            shape((ROWS, DIN), BF16), shape((8, DOUT), F32), shape((8, DOUT), F32),
            shape((8, 128), F32), shape((1, DOUT), F32), shape((TROWS, EMB), F32),
        ),
        in_specs=[anywhere, anywhere, sm, anywhere, anywhere] + [vm] * 7,
        out_specs=(anywhere, vm, vm, vm, vm, vm),
        scratch_shapes=scratch,
        compiler_params=pltpu.CompilerParams(collective_id=0, has_side_effects=True, vmem_limit_bytes=56 << 20),
        name="layer_backward",
    )(
        layer_input, grad_output, row_counts, w_shared, w_scen[0], gain_shared.reshape(1, DOUT), gain_scen,
        saved_mean, saved_rstd, bag_lengths, owner_shard, table_row.reshape(1, ENT),
    )
    return grad_in, dw_shared, dw_scen[None], dgain_shared.reshape(DOUT), dgain_scen, table


def solution(mesh):
    placed = (
        P(("scen", "shard"), None),
        P(("scen", "shard"), None),
        P("scen", "shard"),
        P(),
        P("scen", None, None),
        P(),
        P("scen", None),
        P("scen", None),
        P("scen", None),
        P(("scen", "shard"), None),
        P(("scen", "shard"), None),
        P(("scen", "shard")),
    )
    return jax.shard_map(
        per_device,
        mesh=mesh,
        in_specs=placed,
        out_specs=(
            P(("scen", "shard"), None),
            P("shard", None),
            P("scen", "shard", None),
            P(),
            P("scen", None),
            P("shard", None),
        ),
        check_vma=False,
    )
```

```python
import jax
import jax.numpy as jnp
from jax import lax
from jax.experimental import pallas as pl
from jax.experimental.pallas import tpu as pltpu
from jax.sharding import PartitionSpec as P

F32, BF16, I32 = jnp.float32, jnp.bfloat16, jnp.int32
NZH, NX, NY, NZ = 2, 4, 8, 8
ROWS, DIN, DOUT, EMB, TROWS, ENT, CAP = 256, 1024, 1024, 128, 512, 320, 3
HALF = DOUT // 2
LOAD = 256
PART = NZ * CAP
SLOT = 2 * PART
SLOTS = NY * SLOT
TBLK = TROWS // NX
LONG = NY // 2


def remote(src, dst, send, recv, dev):
    return pltpu.make_async_remote_copy(
        src_ref=src,
        dst_ref=dst,
        send_sem=send,
        recv_sem=recv,
        device_id=dev,
        device_id_type=pl.DeviceIdType.MESH,
    )


class Spread:
    def __init__(self, n, me, dev, src_of, buf, sems, by_place=False):
        self.n, self.me, self.dev, self.src_of, self.buf = n, me, dev, src_of, buf
        self.send, self.recv = sems
        self.by_place = by_place

    def start(self):
        for k in range(1, self.n):
            p = lax.rem(self.me + k, self.n)
            remote(self.src_of(p), self.buf.at[self.me], self.send.at[k], self.recv.at[self.me], self.dev(p)).start()

    def wait(self):
        for k in range(1, self.n):
            q = lax.rem(self.me + k, self.n)
            remote(self.buf.at[q], self.buf.at[q], self.send.at[k], self.recv.at[q], self.dev(q)).wait_recv()

    def finish(self):
        for k in range(1, self.n):
            p = lax.rem(self.me + k, self.n)
            sem = self.send.at[p if self.by_place else k]
            remote(self.src_of(p), self.buf.at[self.me], sem, self.recv.at[self.me], self.dev(p)).wait_send()


def nt(a, b):
    return lax.dot_general(a, b, (((1,), (1,)), ((), ())), preferred_element_type=F32)


def nn(a, b):
    return jnp.dot(a, b, preferred_element_type=F32)


def iota(shape, dim):
    return lax.broadcasted_iota(I32, shape, dim)


def hot(cond):
    return jnp.where(cond, 1.0, 0.0).astype(BF16)


def total(buf, n):
    acc = buf[0].astype(F32)
    for i in range(1, n):
        acc = acc + buf[i].astype(F32)
    return acc


def kernel(
    x_hbm, g_hbm, cnt_ref, ws_hbm, wc_hbm, gs_ref, gc_ref, mean_ref, rstd_ref, len_ref, own_ref, row_ref,
    gi_hbm, dws_ref, dwc_ref, dgs_ref, dgc_ref, tab_ref,
    xb, gb, ws, wc, we, nb, gp, xt, gi,
    stat, stat_c, stat_y, stat_z, fin,
    dw, ring, blk, dz, shx, shz,
    meta, meta_p, pick, ids_s, ids_y, ids_t, ids_z, rows_hot, perm,
    val_s, val_y, val_t, val_z, tab_s, tab_x, tab_h, tab_g, dgx, dgh,
    s_load, s_out, s_core, r_core, s_ring, r_ring,
    *spread_sems,
):
    scen, shard = lax.axis_index("scen"), lax.axis_index("shard")
    zh, x = scen // NX, lax.rem(scen, NX)
    y, z, c = shard // (NZ * 2), lax.rem(shard // 2, NZ), lax.rem(shard, 2)

    def dev_y(p):
        return (scen, (p * NZ + z) * 2 + c)

    def dev_z(p):
        return (scen, (y * NZ + p) * 2 + c)

    def dev_x(p):
        return (zh * NX + p, shard)

    def dev_h(p):
        return (p * NX + x, shard)

    other = 1 - c
    partner = (scen, (y * NZ + z) * 2 + other)

    in_x = pltpu.make_async_copy(x_hbm, xb.at[pl.ds(0, ROWS)], s_load.at[0])
    in_g = pltpu.make_async_copy(g_hbm, gb.at[pl.ds(0, ROWS)], s_load.at[1])
    loads = DOUT // LOAD
    in_w = []
    for j in range(loads):
        cols = pl.ds(j * LOAD, LOAD)
        in_w.append((
            pltpu.make_async_copy(ws_hbm.at[:, cols], ws.at[:, cols], s_load.at[2 + 2 * j]),
            pltpu.make_async_copy(wc_hbm.at[:, cols], wc.at[:, cols], s_load.at[3 + 2 * j]),
        ))
    in_x.start()
    for a, b in in_w[:1]:
        a.start()
        b.start()
    in_g.start()
    for a, b in in_w[1:]:
        a.start()
        b.start()

    barrier = pltpu.get_barrier_semaphore()
    peers = [dev_h(1 - zh)]
    peers += [dev_z(lax.rem(z + k, NZ)) for k in range(1, NZ)]
    peers += [dev_y(lax.rem(y + k, NY)) for k in range(1, NY)]
    peers += [dev_x(lax.rem(x + k, NX)) for k in range(1, NX)]
    peers += [partner]
    for p in peers:
        pl.semaphore_signal(barrier, 1, device_id=p, device_id_type=pl.DeviceIdType.MESH)

    sems = [(spread_sems[2 * i], spread_sems[2 * i + 1]) for i in range(len(spread_sems) // 2)]
    go_stat_y = Spread(NY, y, dev_y, lambda p: stat_y.at[y], stat_y, sems[0])
    go_stat_z = Spread(NZ, z, dev_z, lambda p: stat_z.at[z], stat_z, sems[1])
    go_ids_y = Spread(NY, y, dev_y, lambda p: ids_s.at[p], ids_y, sems[2])
    go_ids_z = Spread(NZ, z, dev_z, lambda p: ids_t.at[p], ids_z, sems[3])
    go_val_y = Spread(NY, y, dev_y, lambda p: val_s.at[p], val_y, sems[4])
    go_val_z = Spread(NZ, z, dev_z, lambda p: val_t.at[p], val_z, sems[5])
    go_dw_z = Spread(NZ, z, dev_z, lambda p: blk.at[p], dz, sems[6], by_place=True)
    go_sh_x = Spread(NX, x, dev_x, lambda p: shx.at[x], shx, sems[7])
    go_sh_h = Spread(NZH, zh, dev_h, lambda p: shz.at[zh], shz, sems[8])
    go_tab_x = Spread(NX, x, dev_x, lambda p: tab_s.at[p], tab_x, sems[9])
    go_tab_h = Spread(NZH, zh, dev_h, lambda p: tab_h.at[zh], tab_h, sems[10])
    go_tab_g = Spread(NX, x, dev_x, lambda p: tab_g.at[x], tab_g, sems[11])
    go_dg_x = Spread(NX, x, dev_x, lambda p: dgx.at[x], dgx, sems[12])
    go_dg_h = Spread(NZH, zh, dev_h, lambda p: dgh.at[zh], dgh, sems[13])
    spreads = [go_stat_y, go_stat_z, go_ids_y, go_ids_z, go_val_y, go_val_z, go_dw_z, go_sh_x, go_sh_h,
               go_tab_x, go_tab_h, go_tab_g, go_dg_x, go_dg_h]
    core_stat = remote(stat.at[other], stat_c, s_core.at[0], r_core.at[0], partner)
    core_fin = remote(fin.at[c], fin.at[c], s_core.at[1], r_core.at[1], partner)
    core_fin_in = remote(fin.at[other], fin.at[other], s_core.at[1], r_core.at[1], partner)
    core_meta = remote(meta, meta_p, s_core.at[2], r_core.at[2], partner)
    core_x = remote(x_hbm, xb.at[pl.ds(ROWS, ROWS)], s_core.at[3], r_core.at[3], partner)
    core_g = remote(g_hbm, gb.at[pl.ds(ROWS, ROWS)], s_core.at[4], r_core.at[4], partner)

    own_hot = jnp.where(own_ref[...] == iota((128, ENT), 0), 1.0, 0.0)
    earlier = nn(own_hot.astype(BF16), hot(iota((ENT, ENT), 0) < iota((ENT, ENT), 1)))
    meta[...] = jnp.zeros_like(meta)
    meta[0:1, 0:ROWS] = len_ref[...].astype(F32)
    meta[1:2, 0:ENT] = own_ref[...].astype(F32) * 4.0 + jnp.sum(earlier * own_hot, axis=0, keepdims=True)
    meta[2:3, 0:ENT] = row_ref[...].astype(F32).reshape(1, ENT)

    count = cnt_ref[0, 0]
    stat[...] = jnp.zeros_like(stat)
    live = iota((ROWS, LOAD), 0) < count
    in_x.wait()
    for j in range(loads):
        cols = pl.ds(j * LOAD, LOAD)
        in_w[j][0].wait()
        in_w[j][1].wait()
        w_j = (ws[:, cols].astype(F32) * wc[:, cols].astype(F32)).astype(BF16)
        we[:, cols] = w_j
        normed = (nn(xb[0:ROWS, :], w_j) - mean_ref[:, cols]) * rstd_ref[:, cols]
        nb[0:ROWS, cols] = normed
        if j == 0:
            in_g.wait()
        masked = jnp.where(live, gb[0:ROWS, cols].astype(F32), 0.0)
        h, at = (j * LOAD) // HALF, (j * LOAD) % HALF
        stat[h, 0:1, at : at + LOAD] = jnp.sum(masked, axis=0, keepdims=True)
        stat[h, 1:2, at : at + LOAD] = jnp.sum(masked * normed, axis=0, keepdims=True)
    cnt_row = jnp.full((1, HALF), count, I32).astype(F32)
    stat[0, 2:3, :] = cnt_row
    stat[1, 2:3, :] = cnt_row

    pl.semaphore_wait(barrier, len(peers))
    core_stat.start()
    core_meta.start()
    core_x.start()
    core_g.start()

    xt_rows = DIN // 2
    choose_i, choose_k = iota((xt_rows, DIN), 0), iota((xt_rows, DIN), 1)
    wanted = ((choose_i >> 5) & 7) * 128 + (choose_i >> 8) * 64 + ((choose_i >> 3) & 3) * 16 + c * 8 + (choose_i & 7)
    choose = hot(choose_k == wanted)

    core_stat.wait_recv()
    stat_y[y] = stat[c] + stat_c[...]
    go_stat_y.start()

    xt[:, 0:ROWS] = nt(choose, xb[0:ROWS, :]).astype(BF16)

    def slots_of(m, src):
        lens = m[0:1, 0:ROWS]
        upto = hot(iota((ROWS, ROWS), 0) <= iota((ROWS, ROWS), 1))
        ends = nn(jnp.broadcast_to(lens, (8, ROWS)).astype(BF16), upto)[0:1]
        entry = iota((ENT, ROWS), 0).astype(F32)
        picker = hot((ends > entry) & (ends - lens <= entry))
        code = m[1:2, 0:ENT].astype(I32)
        owner, place = code >> 2, code & 3
        inside = src * PART + ((owner >> 1) & 7) * CAP + place
        mine = (owner & 1) == c
        slot = jnp.where(mine, (owner >> 4) * SLOT + inside, -1)
        wide = jnp.where(mine, (owner >> 4) * 128 + inside, -1)
        chosen = nn(hot(iota((SLOTS, ENT), 0) == slot), picker).astype(BF16)
        name = m[2:3, 0:ENT].astype(I32) + 1
        part = jnp.where(iota((8, ENT), 0) == 0, name >> 4, name & 15)
        names = nt(part.astype(F32).astype(BF16), hot(iota((NY * 128, ENT), 0) == wide))
        return chosen, names

    core_meta.wait_recv()
    chosen, names = slots_of(meta, c)
    pick[:, 0:ROWS] = chosen
    chosen, names_p = slots_of(meta_p, other)
    pick[:, ROWS : 2 * ROWS] = chosen
    names = names + names_p
    for i in range(NY):
        ids_s[i] = names[:, i * 128 : (i + 1) * 128]

    go_stat_y.wait()
    stat_z[z] = total(stat_y, NY)
    go_stat_z.start()
    ids_y[y] = ids_s[y]
    go_ids_y.start()

    core_x.wait_recv()
    xt[:, ROWS : 2 * ROWS] = nt(choose, xb[ROWS : 2 * ROWS, :]).astype(BF16)
    for j in range(loads):
        cols = pl.ds(j * LOAD, LOAD)
        nb[ROWS : 2 * ROWS, cols] = (nn(xb[ROWS : 2 * ROWS, :], we[:, cols]) - mean_ref[:, cols]) * rstd_ref[:, cols]
    out_i, in_i = iota((SLOTS, SLOTS), 0), iota((SLOTS, SLOTS), 1)
    to_z = (out_i * 1366) >> 16
    in_z = out_i - to_z * SLOT
    six, from_y = in_z >> 3, in_z & 7
    src_c = jnp.where(six >= CAP, 1, 0)
    perm[...] = hot(in_i == from_y * SLOT + src_c * PART + to_z * CAP + six - CAP * src_c)
    core_g.wait_recv()

    go_stat_z.wait()
    fin[c] = total(stat_z, NZ)
    core_fin.start()
    scale = gs_ref[...] * gc_ref[...] * rstd_ref[...]
    core_fin_in.wait_recv()

    sums = [jnp.concatenate([fin[0, i : i + 1, :], fin[1, i : i + 1, :]], axis=1) for i in range(3)]
    sum_dyx = sums[1]
    mean_dy, mean_dyx = sums[0] / sums[2], sums[1] / sums[2]
    count_p = stat_c[2:3, 0:1]

    step = 64
    for i in range(2 * ROWS // step):
        rows = slice(i * step, (i + 1) * step)
        at = iota((step, 1), 0).astype(F32) + float((i * step) % ROWS)
        if i * step < ROWS:
            alive = at < count.astype(F32)
        else:
            alive = at < count_p
        g = gb[rows, :].astype(F32)
        gp[rows, :] = jnp.where(alive, scale * (g - mean_dy - nb[rows, :] * mean_dyx), 0.0).astype(BF16)

    streams = []
    for h in range(2):
        for d in (1, -1):
            streams.append((len(streams), h, d, LONG if (h == 0) == (d == 1) else LONG - 1))

    def hop(s, h, d, n, k):
        src = dw.at[h, lax.rem(y + d * (n - k) + NY, NY)] if k == 0 else ring.at[s, k - 1]
        return remote(src, ring.at[s, k], s_ring.at[s, k], r_ring.at[s, k], dev_y(lax.rem(y + d + NY, NY)))

    quarter = DIN // 4
    for half in range(2):
        for j in range(DOUT // LOAD):
            cols = slice(j * LOAD, (j + 1) * LOAD)
            part = nn(xt[half * quarter : (half + 1) * quarter, :], gp[:, cols])
            dw[half, :, :, cols] = part.astype(BF16).reshape(NY, 32, LOAD)
        for s, h, d, n in streams:
            if h == half:
                hop(s, h, d, n, 0).start()

    def ring_step(k):
        for s, h, d, n in streams:
            if k < n - 1:
                hop(s, h, d, n, k).wait_recv()
                own = dw[h, lax.rem(y + d * (n - k - 1) + NY, NY)]
                ring[s, k] = (ring[s, k].astype(F32) + own.astype(F32)).astype(BF16)
                hop(s, h, d, n, k + 1).start()

    pooled = nt(gp[...], we[0:EMB, :]).astype(BF16)
    val_s[...] = nn(pick[...], pooled).astype(BF16).reshape(NY, SLOT, EMB)
    val_y[y] = val_s[y]
    go_val_y.start()

    dgc_ref[...] = gs_ref[...] * sum_dyx
    gain_term = gc_ref[...] * sum_dyx
    for i in range(8):
        dgx[x, i : i + 1, :] = gain_term[:, i * 128 : (i + 1) * 128]
    go_dg_x.start()

    for j in range(2):
        cols = slice(j * LOAD, (j + 1) * LOAD)
        gi[:, cols] = nt(gp[0:ROWS, :], we[cols, :]).astype(BF16)

    ring_step(0)

    for j in range(2, DIN // LOAD):
        cols = slice(j * LOAD, (j + 1) * LOAD)
        gi[:, cols] = nt(gp[0:ROWS, :], we[cols, :]).astype(BF16)
    out_gi = pltpu.make_async_copy(gi, gi_hbm, s_out.at[0])
    out_gi.start()

    go_ids_y.wait()
    halves = [jnp.concatenate([ids_y[i, r : r + 1, :] for i in range(NY)], axis=0) for r in range(2)]
    q_in, q_out = iota((128, NZ * 128), 0), iota((128, NZ * 128), 1)
    q_z, q_six = q_out >> 7, q_out & 127
    q_src = jnp.where(q_six >= CAP, 1, 0)
    spreader = hot((q_six < 2 * CAP) & (q_in == q_src * PART + q_z * CAP + q_six - CAP * q_src))
    named = nn(jnp.concatenate(halves, axis=0).astype(BF16), spreader)
    named = named[0:8] * 16.0 + named[8:16]
    for i in range(NZ):
        ids_t[i] = named[:, i * 128 : (i + 1) * 128]
    ids_z[z] = ids_t[z]
    go_ids_z.start()

    ring_step(1)

    go_val_y.wait()
    val_t[...] = nn(perm[...], val_y[...].reshape(SLOTS, EMB)).astype(BF16).reshape(NZ, SLOT, EMB)
    val_z[z] = val_t[z]
    go_val_z.start()
    go_dg_x.wait()
    dgh[zh] = total(dgx, NX)
    go_dg_h.start()

    ring_step(2)

    go_ids_z.wait()
    for i in range(NZ):
        for k in range(0, 2 * CAP, 2):
            pair = [ids_z[i][:, t : t + 1] - 1.0 for t in (k, k + 1)]
            at = jnp.concatenate([jnp.broadcast_to(t, (8, TROWS)) for t in pair], axis=0)
            at_row = i * SLOT + k * 8
            rows_hot[at_row : at_row + 16, :] = hot(at == iota((16, TROWS), 1).astype(F32))

    for half in range(2):
        for s, h, d, n in streams:
            if h == half:
                hop(s, h, d, n, n - 1).wait_recv()
        long_s, short_s = (0, 1) if half == 0 else (3, 2)
        summed = ring[long_s, LONG - 1].astype(F32) + dw[half, y].astype(F32) + ring[short_s, LONG - 2].astype(F32)
        for i in range(4):
            b = summed[8 * i : 8 * (i + 1)]
            blk[4 * half + i] = jnp.concatenate([b[:, 0:HALF], b[:, HALF:DOUT]], axis=0).astype(BF16)
        for p in range(4 * half, 4 * half + 4):
            to_p = remote(blk.at[p], dz.at[z], sems[6][0].at[p], sems[6][1].at[z], dev_z(p))
            pl.when(z != p)(to_p.start)
    dz[z] = blk[z]

    go_val_z.wait()
    table = lax.dot_general(
        rows_hot[...], val_z[...].reshape(SLOTS, EMB), (((0,), (0,)), ((), ())), preferred_element_type=F32
    )
    tab_s[...] = table.astype(BF16).reshape(NX, TBLK, EMB)
    tab_x[x] = tab_s[x]
    go_tab_x.start()

    base = pl.multiple_of((y * NZ + z) * 16, 16)

    def block_of(w):
        pair = w[pl.ds(base, 16), :].astype(F32)
        return jnp.where(c == 0, pair[0:8], pair[8:16])

    w_s, w_c = block_of(ws), block_of(wc)

    go_tab_x.wait()
    tab_h[zh] = total(tab_x, NX).astype(BF16)
    go_tab_h.start()

    go_dw_z.wait()
    summed = total(dz, NZ)
    dw_rows = jnp.concatenate([summed[0:8], summed[8:16]], axis=1)
    shared = dw_rows * w_c
    shx[x] = jnp.concatenate([shared[:, 0:HALF], shared[:, HALF:DOUT]], axis=0).astype(BF16)
    go_sh_x.start()
    dwc_ref[...] = dw_rows * w_s

    go_sh_x.wait()
    shz[zh] = total(shx, NX).astype(BF16)
    go_sh_h.start()

    go_dg_h.wait()
    dgs_ref[...] = total(dgh, NZH)

    go_tab_h.wait()
    tab_g[x] = total(tab_h, NZH).astype(BF16)
    go_tab_g.start()

    for sp in spreads:
        if sp not in (go_sh_h, go_tab_g):
            sp.finish()
    for cp in (core_stat, core_fin, core_meta, core_x, core_g):
        cp.wait_send()
    for s, h, d, n in streams:
        for k in range(n):
            hop(s, h, d, n, k).wait_send()
    out_gi.wait()

    go_sh_h.wait()
    summed = total(shz, NZH)
    dws_ref[...] = jnp.concatenate([summed[0:8], summed[8:16]], axis=1)

    go_tab_g.wait()
    tab_ref[...] = tab_g[...].astype(F32).reshape(TROWS, EMB)

    for sp in (go_sh_h, go_tab_g):
        sp.finish()


def hand_over(*refs):
    for i in range(6):
        refs[6 + i][...] = refs[i][...]


def per_device(*args):
    (layer_input, grad_output, row_counts, w_shared, w_scen, gain_shared, gain_scen,
     saved_mean, saved_rstd, bag_lengths, owner_shard, table_row) = args
    vm, sm, anywhere = (pl.BlockSpec(memory_space=m) for m in (pltpu.VMEM, pltpu.SMEM, pl.ANY))
    dma = pltpu.SemaphoreType.DMA
    V = pltpu.VMEM
    sizes = [NY, NZ, NY, NZ, NY, NZ, NZ, NX, NZH, NX, NZH, NX, NX, NZH]
    scratch = [
        V((2 * ROWS, DIN), BF16), V((2 * ROWS, DOUT), BF16), V((DIN, DOUT), BF16), V((DIN, DOUT), BF16),
        V((DIN, DOUT), BF16), V((2 * ROWS, DOUT), F32), V((2 * ROWS, DOUT), BF16), V((DIN // 2, 2 * ROWS), BF16),
        V((ROWS, DIN), BF16),
        V((2, 8, HALF), F32), V((8, HALF), F32), V((NY, 8, HALF), F32), V((NZ, 8, HALF), F32), V((2, 8, HALF), F32),
        V((2, NY, 32, DOUT), BF16), V((4, LONG, 32, DOUT), BF16), V((NZ, 16, HALF), BF16),
        V((NZ, 16, HALF), BF16), V((NX, 16, HALF), BF16), V((NZH, 16, HALF), BF16),
        V((8, 512), F32), V((8, 512), F32), V((SLOTS, 2 * ROWS), BF16), V((NY, 8, 128), F32), V((NY, 8, 128), F32),
        V((NZ, 8, 128), F32), V((NZ, 8, 128), F32), V((SLOTS, TROWS), BF16), V((SLOTS, SLOTS), BF16),
        V((NY, SLOT, EMB), BF16), V((NY, SLOT, EMB), BF16), V((NZ, SLOT, EMB), BF16), V((NZ, SLOT, EMB), BF16),
        V((NX, TBLK, EMB), BF16), V((NX, TBLK, EMB), BF16), V((NZH, TBLK, EMB), BF16), V((NX, TBLK, EMB), BF16),
        V((NX, 8, 128), F32), V((NZH, 8, 128), F32),
        dma((2 + 2 * (DOUT // LOAD),)), dma((1,)), dma((5,)), dma((5,)), dma((4, LONG)), dma((4, LONG)),
    ]
    for n in sizes:
        scratch += [dma((n,)), dma((n,))]
    shape = jax.ShapeDtypeStruct
    grad_in, dw_shared, dw_scen, dgain_shared, dgain_scen, table = pl.pallas_call(
        kernel,
        out_shape=(
            shape((ROWS, DIN), BF16), shape((8, DOUT), F32), shape((8, DOUT), F32),
            shape((8, 128), F32), shape((1, DOUT), F32), shape((TROWS, EMB), F32),
        ),
        in_specs=[anywhere, anywhere, sm, anywhere, anywhere] + [vm] * 7,
        out_specs=(anywhere, vm, vm, vm, vm, vm),
        scratch_shapes=scratch,
        compiler_params=pltpu.CompilerParams(collective_id=0, has_side_effects=True, vmem_limit_bytes=56 << 20),
        name="layer_backward",
    )(
        layer_input, grad_output, row_counts, w_shared, w_scen[0], gain_shared.reshape(1, DOUT), gain_scen,
        saved_mean, saved_rstd, bag_lengths, owner_shard.reshape(1, ENT), table_row,
    )
    results = (grad_in, dw_shared, dw_scen, dgain_shared, dgain_scen, table)
    grad_in, dw_shared, dw_scen, dgain_shared, dgain_scen, table = pl.pallas_call(
        hand_over,
        out_shape=tuple(shape(r.shape, r.dtype) for r in results),
        in_specs=[vm] * 6,
        out_specs=(vm,) * 6,
        compiler_params=pltpu.CompilerParams(vmem_limit_bytes=60 << 20),
        name="hand_over",
    )(*results)
    return grad_in, dw_shared, dw_scen[None], dgain_shared.reshape(DOUT), dgain_scen, table


def solution(mesh):
    placed = (
        P(("scen", "shard"), None),
        P(("scen", "shard"), None),
        P("scen", "shard"),
        P(),
        P("scen", None, None),
        P(),
        P("scen", None),
        P("scen", None),
        P("scen", None),
        P(("scen", "shard"), None),
        P(("scen", "shard"), None),
        P(("scen", "shard")),
    )
    return jax.shard_map(
        per_device,
        mesh=mesh,
        in_specs=placed,
        out_specs=(
            P(("scen", "shard"), None),
            P("shard", None),
            P("scen", "shard", None),
            P(),
            P("scen", None),
            P("shard", None),
        ),
        check_vma=False,
    )
```

```python
import jax
import jax.numpy as jnp
from jax import lax
from jax.experimental import pallas as pl
from jax.experimental.pallas import tpu as pltpu
from jax.sharding import PartitionSpec as P

F32, BF16, I32 = jnp.float32, jnp.bfloat16, jnp.int32
NZH, NX, NY, NZ = 2, 4, 8, 8
ROWS, DIN, DOUT, EMB, TROWS, ENT, CAP = 256, 1024, 1024, 128, 512, 320, 3
HALF = DOUT // 2
LOAD = 256
PART = NZ * CAP
SLOT = 2 * PART
SLOTS = NY * SLOT
TBLK = TROWS // NX
LONG = NY // 2


def remote(src, dst, send, recv, dev):
    return pltpu.make_async_remote_copy(
        src_ref=src,
        dst_ref=dst,
        send_sem=send,
        recv_sem=recv,
        device_id=dev,
        device_id_type=pl.DeviceIdType.MESH,
    )


def far_first(n, me):
    return [lax.rem(me + k, n) for k in sorted(range(1, n), key=lambda k: -min(k, n - k))]


def far_line(n, me):
    upper = me // (n // 2)
    order = []
    for i in range(n - 1):
        down = n - 1 - i - (me + i + 1) // n
        up = i + (i - me + n) // n
        order.append((1 - upper) * down + upper * up)
    return order


class Spread:
    def __init__(self, n, me, dev, src_of, buf, sems, by_place=False, line=False):
        self.n, self.me, self.dev, self.src_of, self.buf = n, me, dev, src_of, buf
        self.send, self.recv = sems
        self.by_place = by_place
        self.order = far_line(n, me) if line else far_first(n, me)

    def sends(self):
        for i, p in enumerate(self.order):
            sem = self.send.at[p if self.by_place else i + 1]
            yield remote(self.src_of(p), self.buf.at[self.me], sem, self.recv.at[self.me], self.dev(p))

    def start(self):
        for cp in self.sends():
            cp.start()

    def wait(self):
        for k in range(1, self.n):
            q = lax.rem(self.me + k, self.n)
            remote(self.buf.at[q], self.buf.at[q], self.send.at[k], self.recv.at[q], self.dev(q)).wait_recv()

    def finish(self):
        for cp in self.sends():
            cp.wait_send()


def nt(a, b):
    return lax.dot_general(a, b, (((1,), (1,)), ((), ())), preferred_element_type=F32)


def nn(a, b):
    return jnp.dot(a, b, preferred_element_type=F32)


def iota(shape, dim):
    return lax.broadcasted_iota(I32, shape, dim)


def hot(cond):
    return jnp.where(cond, 1.0, 0.0).astype(BF16)


def total(buf, n):
    acc = buf[0].astype(F32)
    for i in range(1, n):
        acc = acc + buf[i].astype(F32)
    return acc


def kernel(
    x_hbm, g_hbm, cnt_ref, ws_hbm, wc_hbm, gs_ref, gc_ref, mean_ref, rstd_ref, len_ref, own_ref, row_ref,
    gi_hbm, dws_ref, dwc_ref, dgs_ref, dgc_ref, tab_ref,
    xb, gb, ws, wc, we, nb, gp, xt, gi,
    stat, stat_c, stat_y, stat_z, fin,
    dw, ring, blk, dz, shx, shz,
    meta, meta_p, pick, ids_s, ids_y, ids_t, ids_z, rows_hot, perm,
    val_s, val_y, val_t, val_z, tab_s, tab_x, tab_h, tab_g, dgx, dgh,
    s_load, s_out, s_core, r_core, s_ring, r_ring,
    *spread_sems,
):
    scen, shard = lax.axis_index("scen"), lax.axis_index("shard")
    zh, x = scen // NX, lax.rem(scen, NX)
    y, z, c = shard // (NZ * 2), lax.rem(shard // 2, NZ), lax.rem(shard, 2)

    def dev_y(p):
        return (scen, (p * NZ + z) * 2 + c)

    def dev_z(p):
        return (scen, (y * NZ + p) * 2 + c)

    def dev_x(p):
        return (zh * NX + p, shard)

    def dev_h(p):
        return (p * NX + x, shard)

    other = 1 - c
    partner = (scen, (y * NZ + z) * 2 + other)

    barrier = pltpu.get_barrier_semaphore()
    peers = [dev_h(1 - zh)]
    peers += [dev_z(lax.rem(z + k, NZ)) for k in range(1, NZ)]
    peers += [dev_y(lax.rem(y + k, NY)) for k in range(1, NY)]
    peers += [dev_x(lax.rem(x + k, NX)) for k in range(1, NX)]
    peers += [partner]
    for p in peers:
        pl.semaphore_signal(barrier, 1, device_id=p, device_id_type=pl.DeviceIdType.MESH)

    in_x = pltpu.make_async_copy(x_hbm, xb.at[pl.ds(0, ROWS)], s_load.at[0])
    in_g = pltpu.make_async_copy(g_hbm, gb.at[pl.ds(0, ROWS)], s_load.at[1])
    loads = DOUT // LOAD
    in_w = []
    for j in range(loads):
        cols = pl.ds(j * LOAD, LOAD)
        in_w.append((
            pltpu.make_async_copy(ws_hbm.at[:, cols], ws.at[:, cols], s_load.at[2 + 2 * j]),
            pltpu.make_async_copy(wc_hbm.at[:, cols], wc.at[:, cols], s_load.at[3 + 2 * j]),
        ))
    in_x.start()
    for a, b in in_w[:1]:
        a.start()
        b.start()
    in_g.start()
    for a, b in in_w[1:]:
        a.start()
        b.start()

    sems = [(spread_sems[2 * i], spread_sems[2 * i + 1]) for i in range(len(spread_sems) // 2)]
    go_stat_y = Spread(NY, y, dev_y, lambda p: stat_y.at[y], stat_y, sems[0])
    go_stat_z = Spread(NZ, z, dev_z, lambda p: stat_z.at[z], stat_z, sems[1], line=True)
    go_ids_y = Spread(NY, y, dev_y, lambda p: ids_s.at[p], ids_y, sems[2])
    go_ids_z = Spread(NZ, z, dev_z, lambda p: ids_t.at[p], ids_z, sems[3], line=True)
    go_val_y = Spread(NY, y, dev_y, lambda p: val_s.at[p], val_y, sems[4])
    go_val_z = Spread(NZ, z, dev_z, lambda p: val_t.at[p], val_z, sems[5], line=True)
    go_dw_z = Spread(NZ, z, dev_z, lambda p: blk.at[p], dz, sems[6], by_place=True, line=True)
    go_sh_x = Spread(NX, x, dev_x, lambda p: shx.at[x], shx, sems[7])
    go_sh_h = Spread(NZH, zh, dev_h, lambda p: shz.at[zh], shz, sems[8])
    go_tab_x = Spread(NX, x, dev_x, lambda p: tab_s.at[p], tab_x, sems[9])
    go_tab_h = Spread(NZH, zh, dev_h, lambda p: tab_h.at[zh], tab_h, sems[10])
    go_tab_g = Spread(NX, x, dev_x, lambda p: tab_g.at[x], tab_g, sems[11])
    go_dg_x = Spread(NX, x, dev_x, lambda p: dgx.at[x], dgx, sems[12])
    go_dg_h = Spread(NZH, zh, dev_h, lambda p: dgh.at[zh], dgh, sems[13])
    spreads = [go_stat_y, go_stat_z, go_ids_y, go_ids_z, go_val_y, go_val_z, go_dw_z, go_sh_x, go_sh_h,
               go_tab_x, go_tab_h, go_tab_g, go_dg_x, go_dg_h]
    core_stat = remote(stat.at[other], stat_c, s_core.at[0], r_core.at[0], partner)
    core_fin = remote(fin.at[c], fin.at[c], s_core.at[1], r_core.at[1], partner)
    core_fin_in = remote(fin.at[other], fin.at[other], s_core.at[1], r_core.at[1], partner)
    core_meta = remote(meta, meta_p, s_core.at[2], r_core.at[2], partner)
    core_x = remote(x_hbm, xb.at[pl.ds(ROWS, ROWS)], s_core.at[3], r_core.at[3], partner)
    core_g = remote(g_hbm, gb.at[pl.ds(ROWS, ROWS)], s_core.at[4], r_core.at[4], partner)

    own_hot = jnp.where(own_ref[...] == iota((128, ENT), 0), 1.0, 0.0)
    earlier = nn(own_hot.astype(BF16), hot(iota((ENT, ENT), 0) < iota((ENT, ENT), 1)))
    meta[...] = jnp.zeros_like(meta)
    meta[0:1, 0:ROWS] = len_ref[...].astype(F32)
    meta[1:2, 0:ENT] = own_ref[...].astype(F32) * 4.0 + jnp.sum(earlier * own_hot, axis=0, keepdims=True)
    meta[2:3, 0:ENT] = row_ref[...].astype(F32).reshape(1, ENT)

    def slots_of(m, src):
        lens = m[0:1, 0:ROWS]
        upto = hot(iota((ROWS, ROWS), 0) <= iota((ROWS, ROWS), 1))
        ends = nn(jnp.broadcast_to(lens, (8, ROWS)).astype(BF16), upto)[0:1]
        entry = iota((ENT, ROWS), 0).astype(F32)
        picker = hot((ends > entry) & (ends - lens <= entry))
        code = m[1:2, 0:ENT].astype(I32)
        owner, place = code >> 2, code & 3
        inside = src * PART + ((owner >> 1) & 7) * CAP + place
        mine = (owner & 1) == c
        slot = jnp.where(mine, (owner >> 4) * SLOT + inside, -1)
        wide = jnp.where(mine, (owner >> 4) * 128 + inside, -1)
        chosen = nn(hot(iota((SLOTS, ENT), 0) == slot), picker).astype(BF16)
        name = m[2:3, 0:ENT].astype(I32) + 1
        part = jnp.where(iota((8, ENT), 0) == 0, name >> 4, name & 15)
        names = nt(part.astype(F32).astype(BF16), hot(iota((NY * 128, ENT), 0) == wide))
        return chosen, names

    chosen, names = slots_of(meta, c)
    pick[:, 0:ROWS] = chosen

    count = cnt_ref[0, 0]
    stat[...] = jnp.zeros_like(stat)
    live = iota((ROWS, LOAD), 0) < count
    in_x.wait()
    for j in range(loads):
        cols = pl.ds(j * LOAD, LOAD)
        in_w[j][0].wait()
        in_w[j][1].wait()
        w_j = (ws[:, cols].astype(F32) * wc[:, cols].astype(F32)).astype(BF16)
        we[:, cols] = w_j
        normed = (nn(xb[0:ROWS, :], w_j) - mean_ref[:, cols]) * rstd_ref[:, cols]
        nb[0:ROWS, cols] = normed
        if j == 0:
            in_g.wait()
        masked = jnp.where(live, gb[0:ROWS, cols].astype(F32), 0.0)
        h, at = (j * LOAD) // HALF, (j * LOAD) % HALF
        stat[h, 0:1, at : at + LOAD] = jnp.sum(masked, axis=0, keepdims=True)
        stat[h, 1:2, at : at + LOAD] = jnp.sum(masked * normed, axis=0, keepdims=True)
    cnt_row = jnp.full((1, HALF), count, I32).astype(F32)
    stat[0, 2:3, :] = cnt_row
    stat[1, 2:3, :] = cnt_row

    pl.semaphore_wait(barrier, len(peers))
    core_stat.start()
    core_meta.start()
    core_x.start()
    core_g.start()

    xt_rows = DIN // 2
    choose_i, choose_k = iota((xt_rows, DIN), 0), iota((xt_rows, DIN), 1)
    wanted = ((choose_i >> 5) & 7) * 128 + (choose_i >> 8) * 64 + ((choose_i >> 3) & 3) * 16 + c * 8 + (choose_i & 7)
    choose = hot(choose_k == wanted)

    core_stat.wait_recv()
    stat_y[y] = stat[c] + stat_c[...]
    go_stat_y.start()

    xt[:, 0:ROWS] = nt(choose, xb[0:ROWS, :]).astype(BF16)

    core_meta.wait_recv()
    chosen, names_p = slots_of(meta_p, other)
    pick[:, ROWS : 2 * ROWS] = chosen
    names = names + names_p
    for i in range(NY):
        ids_s[i] = names[:, i * 128 : (i + 1) * 128]

    go_stat_y.wait()
    stat_z[z] = total(stat_y, NY)
    go_stat_z.start()
    ids_y[y] = ids_s[y]
    go_ids_y.start()

    core_x.wait_recv()
    xt[:, ROWS : 2 * ROWS] = nt(choose, xb[ROWS : 2 * ROWS, :]).astype(BF16)
    for j in range(loads):
        cols = pl.ds(j * LOAD, LOAD)
        nb[ROWS : 2 * ROWS, cols] = (nn(xb[ROWS : 2 * ROWS, :], we[:, cols]) - mean_ref[:, cols]) * rstd_ref[:, cols]
    core_g.wait_recv()

    go_stat_z.wait()
    fin[c] = total(stat_z, NZ)
    core_fin.start()
    scale = gs_ref[...] * gc_ref[...] * rstd_ref[...]
    core_fin_in.wait_recv()

    sums = [jnp.concatenate([fin[0, i : i + 1, :], fin[1, i : i + 1, :]], axis=1) for i in range(3)]
    sum_dyx = sums[1]
    mean_dy, mean_dyx = sums[0] / sums[2], sums[1] / sums[2]
    count_p = stat_c[2:3, 0:1]

    step = 64
    for i in range(2 * ROWS // step):
        rows = slice(i * step, (i + 1) * step)
        at = iota((step, 1), 0).astype(F32) + float((i * step) % ROWS)
        if i * step < ROWS:
            alive = at < count.astype(F32)
        else:
            alive = at < count_p
        g = gb[rows, :].astype(F32)
        gp[rows, :] = jnp.where(alive, scale * (g - mean_dy - nb[rows, :] * mean_dyx), 0.0).astype(BF16)

    streams = []
    for h in range(2):
        for d in (1, -1):
            streams.append((len(streams), h, d, LONG if (h == 0) == (d == 1) else LONG - 1))

    def hop(s, h, d, n, k):
        src = dw.at[h, lax.rem(y + d * (n - k) + NY, NY)] if k == 0 else ring.at[s, k - 1]
        return remote(src, ring.at[s, k], s_ring.at[s, k], r_ring.at[s, k], dev_y(lax.rem(y + d + NY, NY)))

    quarter = DIN // 4
    for half in range(2):
        for j in range(DOUT // LOAD):
            cols = slice(j * LOAD, (j + 1) * LOAD)
            part = nn(xt[half * quarter : (half + 1) * quarter, :], gp[:, cols])
            dw[half, :, :, cols] = part.astype(BF16).reshape(NY, 32, LOAD)
        for s, h, d, n in streams:
            if h == half:
                hop(s, h, d, n, 0).start()

    def ring_step(k):
        for s, h, d, n in streams:
            if k < n - 1:
                hop(s, h, d, n, k).wait_recv()
                own = dw[h, lax.rem(y + d * (n - k - 1) + NY, NY)]
                ring[s, k] = (ring[s, k].astype(F32) + own.astype(F32)).astype(BF16)
                hop(s, h, d, n, k + 1).start()

    pooled = nt(gp[...], we[0:EMB, :]).astype(BF16)
    val_s[...] = nn(pick[...], pooled).astype(BF16).reshape(NY, SLOT, EMB)
    val_y[y] = val_s[y]
    go_val_y.start()
    out_i, in_i = iota((SLOTS, SLOTS), 0), iota((SLOTS, SLOTS), 1)
    to_z = (out_i * 1366) >> 16
    in_z = out_i - to_z * SLOT
    six, from_y = in_z >> 3, in_z & 7
    src_c = jnp.where(six >= CAP, 1, 0)
    perm[...] = hot(in_i == from_y * SLOT + src_c * PART + to_z * CAP + six - CAP * src_c)

    dgc_ref[...] = gs_ref[...] * sum_dyx
    gain_term = gc_ref[...] * sum_dyx
    for i in range(8):
        dgx[x, i : i + 1, :] = gain_term[:, i * 128 : (i + 1) * 128]
    go_dg_x.start()

    for j in range(2):
        cols = slice(j * LOAD, (j + 1) * LOAD)
        gi[:, cols] = nt(gp[0:ROWS, :], we[cols, :]).astype(BF16)

    ring_step(0)

    for j in range(2, DIN // LOAD):
        cols = slice(j * LOAD, (j + 1) * LOAD)
        gi[:, cols] = nt(gp[0:ROWS, :], we[cols, :]).astype(BF16)
    out_gi = pltpu.make_async_copy(gi, gi_hbm, s_out.at[0])
    out_gi.start()

    go_ids_y.wait()
    halves = [jnp.concatenate([ids_y[i, r : r + 1, :] for i in range(NY)], axis=0) for r in range(2)]
    q_in, q_out = iota((128, NZ * 128), 0), iota((128, NZ * 128), 1)
    q_z, q_six = q_out >> 7, q_out & 127
    q_src = jnp.where(q_six >= CAP, 1, 0)
    spreader = hot((q_six < 2 * CAP) & (q_in == q_src * PART + q_z * CAP + q_six - CAP * q_src))
    named = nn(jnp.concatenate(halves, axis=0).astype(BF16), spreader)
    named = named[0:8] * 16.0 + named[8:16]
    for i in range(NZ):
        ids_t[i] = named[:, i * 128 : (i + 1) * 128]
    ids_z[z] = ids_t[z]
    go_ids_z.start()

    ring_step(1)

    go_val_y.wait()
    val_t[...] = nn(perm[...], val_y[...].reshape(SLOTS, EMB)).astype(BF16).reshape(NZ, SLOT, EMB)
    val_z[z] = val_t[z]
    go_val_z.start()
    go_dg_x.wait()
    dgh[zh] = total(dgx, NX)
    go_dg_h.start()

    ring_step(2)

    go_ids_z.wait()
    for i in range(NZ):
        for k in range(0, 2 * CAP, 2):
            pair = [ids_z[i][:, t : t + 1] - 1.0 for t in (k, k + 1)]
            at = jnp.concatenate([jnp.broadcast_to(t, (8, TROWS)) for t in pair], axis=0)
            at_row = i * SLOT + k * 8
            rows_hot[at_row : at_row + 16, :] = hot(at == iota((16, TROWS), 1).astype(F32))

    for half in range(2):
        for s, h, d, n in streams:
            if h == half:
                hop(s, h, d, n, n - 1).wait_recv()
        long_s, short_s = (0, 1) if half == 0 else (3, 2)
        summed = ring[long_s, LONG - 1].astype(F32) + dw[half, y].astype(F32) + ring[short_s, LONG - 2].astype(F32)
        for i in range(4):
            b = summed[8 * i : 8 * (i + 1)]
            blk[4 * half + i] = jnp.concatenate([b[:, 0:HALF], b[:, HALF:DOUT]], axis=0).astype(BF16)
        for p in range(4 * half, 4 * half + 4):
            to_p = remote(blk.at[p], dz.at[z], sems[6][0].at[p], sems[6][1].at[z], dev_z(p))
            pl.when(z != p)(to_p.start)
    dz[z] = blk[z]

    go_val_z.wait()
    table = lax.dot_general(
        rows_hot[...], val_z[...].reshape(SLOTS, EMB), (((0,), (0,)), ((), ())), preferred_element_type=F32
    )
    tab_s[...] = table.astype(BF16).reshape(NX, TBLK, EMB)
    tab_x[x] = tab_s[x]
    go_tab_x.start()

    base = pl.multiple_of((y * NZ + z) * 16, 16)

    def block_of(w):
        pair = w[pl.ds(base, 16), :].astype(F32)
        return jnp.where(c == 0, pair[0:8], pair[8:16])

    w_s, w_c = block_of(ws), block_of(wc)

    go_tab_x.wait()
    tab_h[zh] = total(tab_x, NX).astype(BF16)
    go_tab_h.start()

    go_dw_z.wait()
    summed = total(dz, NZ)
    dw_rows = jnp.concatenate([summed[0:8], summed[8:16]], axis=1)
    shared = dw_rows * w_c
    shx[x] = jnp.concatenate([shared[:, 0:HALF], shared[:, HALF:DOUT]], axis=0).astype(BF16)
    go_sh_x.start()
    dwc_ref[...] = dw_rows * w_s

    go_sh_x.wait()
    shz[zh] = total(shx, NX).astype(BF16)
    go_sh_h.start()

    go_dg_h.wait()
    dgs_ref[...] = total(dgh, NZH)

    go_tab_h.wait()
    tab_g[x] = total(tab_h, NZH).astype(BF16)
    go_tab_g.start()

    for sp in spreads:
        if sp not in (go_sh_h, go_tab_g):
            sp.finish()
    for cp in (core_stat, core_fin, core_meta, core_x, core_g):
        cp.wait_send()
    for s, h, d, n in streams:
        for k in range(n):
            hop(s, h, d, n, k).wait_send()
    out_gi.wait()

    go_sh_h.wait()
    summed = total(shz, NZH)
    dws_ref[...] = jnp.concatenate([summed[0:8], summed[8:16]], axis=1)

    go_tab_g.wait()
    tab_ref[...] = tab_g[...].astype(F32).reshape(TROWS, EMB)

    for sp in (go_sh_h, go_tab_g):
        sp.finish()


def hand_over(*refs):
    for i in range(6):
        refs[6 + i][...] = refs[i][...]


def per_device(*args):
    (layer_input, grad_output, row_counts, w_shared, w_scen, gain_shared, gain_scen,
     saved_mean, saved_rstd, bag_lengths, owner_shard, table_row) = args
    vm, sm, anywhere = (pl.BlockSpec(memory_space=m) for m in (pltpu.VMEM, pltpu.SMEM, pl.ANY))
    dma = pltpu.SemaphoreType.DMA
    V = pltpu.VMEM
    sizes = [NY, NZ, NY, NZ, NY, NZ, NZ, NX, NZH, NX, NZH, NX, NX, NZH]
    scratch = [
        V((2 * ROWS, DIN), BF16), V((2 * ROWS, DOUT), BF16), V((DIN, DOUT), BF16), V((DIN, DOUT), BF16),
        V((DIN, DOUT), BF16), V((2 * ROWS, DOUT), F32), V((2 * ROWS, DOUT), BF16), V((DIN // 2, 2 * ROWS), BF16),
        V((ROWS, DIN), BF16),
        V((2, 8, HALF), F32), V((8, HALF), F32), V((NY, 8, HALF), F32), V((NZ, 8, HALF), F32), V((2, 8, HALF), F32),
        V((2, NY, 32, DOUT), BF16), V((4, LONG, 32, DOUT), BF16), V((NZ, 16, HALF), BF16),
        V((NZ, 16, HALF), BF16), V((NX, 16, HALF), BF16), V((NZH, 16, HALF), BF16),
        V((8, 512), F32), V((8, 512), F32), V((SLOTS, 2 * ROWS), BF16), V((NY, 8, 128), F32), V((NY, 8, 128), F32),
        V((NZ, 8, 128), F32), V((NZ, 8, 128), F32), V((SLOTS, TROWS), BF16), V((SLOTS, SLOTS), BF16),
        V((NY, SLOT, EMB), BF16), V((NY, SLOT, EMB), BF16), V((NZ, SLOT, EMB), BF16), V((NZ, SLOT, EMB), BF16),
        V((NX, TBLK, EMB), BF16), V((NX, TBLK, EMB), BF16), V((NZH, TBLK, EMB), BF16), V((NX, TBLK, EMB), BF16),
        V((NX, 8, 128), F32), V((NZH, 8, 128), F32),
        dma((2 + 2 * (DOUT // LOAD),)), dma((1,)), dma((5,)), dma((5,)), dma((4, LONG)), dma((4, LONG)),
    ]
    for n in sizes:
        scratch += [dma((n,)), dma((n,))]
    shape = jax.ShapeDtypeStruct
    grad_in, dw_shared, dw_scen, dgain_shared, dgain_scen, table = pl.pallas_call(
        kernel,
        out_shape=(
            shape((ROWS, DIN), BF16), shape((8, DOUT), F32), shape((8, DOUT), F32),
            shape((8, 128), F32), shape((1, DOUT), F32), shape((TROWS, EMB), F32),
        ),
        in_specs=[anywhere, anywhere, sm, anywhere, anywhere] + [vm] * 7,
        out_specs=(anywhere, vm, vm, vm, vm, vm),
        scratch_shapes=scratch,
        compiler_params=pltpu.CompilerParams(collective_id=0, has_side_effects=True, vmem_limit_bytes=56 << 20),
        name="layer_backward",
    )(
        layer_input, grad_output, row_counts, w_shared, w_scen[0], gain_shared.reshape(1, DOUT), gain_scen,
        saved_mean, saved_rstd, bag_lengths, owner_shard.reshape(1, ENT), table_row,
    )
    results = (grad_in, dw_shared, dw_scen, dgain_shared, dgain_scen, table)
    grad_in, dw_shared, dw_scen, dgain_shared, dgain_scen, table = pl.pallas_call(
        hand_over,
        out_shape=tuple(shape(r.shape, r.dtype) for r in results),
        in_specs=[vm] * 6,
        out_specs=(vm,) * 6,
        compiler_params=pltpu.CompilerParams(vmem_limit_bytes=60 << 20),
        name="hand_over",
    )(*results)
    return grad_in, dw_shared, dw_scen[None], dgain_shared.reshape(DOUT), dgain_scen, table


def solution(mesh):
    placed = (
        P(("scen", "shard"), None),
        P(("scen", "shard"), None),
        P("scen", "shard"),
        P(),
        P("scen", None, None),
        P(),
        P("scen", None),
        P("scen", None),
        P("scen", None),
        P(("scen", "shard"), None),
        P(("scen", "shard"), None),
        P(("scen", "shard")),
    )
    return jax.shard_map(
        per_device,
        mesh=mesh,
        in_specs=placed,
        out_specs=(
            P(("scen", "shard"), None),
            P("shard", None),
            P("scen", "shard", None),
            P(),
            P("scen", None),
            P("shard", None),
        ),
        check_vma=False,
    )
```
